32 devices in a mesh: groups: 2 (over y), ctx: 4 (over z), dp: 2 (over x), head: 2 (over core).
Axes of the slice: x: 2, y: 2, z: 4, core: 2. Of those that a mesh axis runs over, the one named last changes fastest.
Arguments:
- queries: bfloat16 [4, 1024, 2048], P(('groups', 'dp'), 'ctx', 'head'), parts along dimension 0, may hold values from -6.2 to 6.2
- keys: bfloat16 [4, 1024, 512], P(('groups', 'dp'), 'ctx', 'head'), parts along dimension 0, may hold values from -6.2 to 6.2
- values: bfloat16 [4, 1024, 512], P(('groups', 'dp'), 'ctx', 'head'), parts along dimension 0, may hold values from -6 to 6
- tok_ids: int32 [4, 1024], P(('groups', 'dp'), 'ctx'), parts along dimension 0, may hold values from 0 to 15, never falling along the last dimension, each value on 1 to 128 neighbouring positions
- vis_start: int32 [4, 4], P(('groups', 'dp'), 'ctx'), parts along dimension 0, may hold values from 0 to 3, as said below
- out_weight: bfloat16 [4096, 2048], P('dp', 'head'), may hold values from -0.125 to 0.125
- grad_out: bfloat16 [4, 1024, 4096], P(('groups', 'dp'), 'ctx'), parts along dimension 0, may hold values from -6 to 6
Outputs:
- grad_q: bfloat16 [4, 1024, 2048], P(('groups', 'dp'), 'ctx', 'head'), parts along dimension 0
- key_gradient: bfloat16 [4, 1024, 512], P(('groups', 'dp'), 'ctx', 'head'), parts along dimension 0
- value_gradient: bfloat16 [4, 1024, 512], P(('groups', 'dp'), 'ctx', 'head'), parts along dimension 0
- weight_grad: bfloat16 [8192, 2048], P(('groups', 'dp'), 'head'), parts along dimension 0
The draws below stay inside these ranges and needn't reach their ends.
There are 2 independent parts, one for each index of `groups`. The reference program is written for one: setup_inputs(seed, part) draws one part's arguments, and reference() takes and returns one part's arrays. A program takes and returns all parts, laid end to end along the dimension named above; an argument that names none is the same for every part. Nothing has to cross between parts.
Inputs may be any that keep to these rules, and one draw needn't show every extreme that they name: vis_start[b, j] lies between 0 and j, and vis_start[b, 0] is 0.
All inputs are finite; a program needn't handle non-finite values.
Results may differ from the reference program's by a relative error of at most 0.011.
Values may be sent and summed in bfloat16 or wider, within the bound.
No kernel may reach another device: no remote copies, remote signals or barrier semaphores. Data moves between devices by JAX's collectives and lax.ppermute only.
A program may use at most 128 MiB of HBM per device.

```python
import math
import jax
import jax.numpy as jnp
import numpy as np
from jax import lax

D = 4096
QUERY_HEADS = 16
KEY_VALUE_HEADS = 4
HEAD_SIZE = 128
SUMMARY_TOKENS = 64
SEGMENT_TOKENS = 256
DOC_COUNT = 2
DOC_TOKENS = 1024
N_CTX = 4


def draw_keys(key, part):
    key = jax.random.fold_in(key, 11)
    base_offset = jnp.clip(jax.random.normal(key, (DOC_COUNT, DOC_TOKENS, KEY_VALUE_HEADS * HEAD_SIZE), jnp.float32), -6.0, 6.0)
    return base_offset.astype(jnp.bfloat16)


def draw_queries(key, part):
    key = jax.random.fold_in(key, 12)
    base_offset = jnp.clip(jax.random.normal(key, (DOC_COUNT, DOC_TOKENS, QUERY_HEADS * HEAD_SIZE), jnp.float32), -6.0, 6.0)
    return base_offset.astype(jnp.bfloat16)


def draw_vis_start(key, part):
    key = jax.random.fold_in(key, 13)
    upper = jnp.arange(N_CTX, dtype=jnp.int32) + 1
    drawn = jax.random.randint(key, (DOC_COUNT, N_CTX), 0, upper[None, :], dtype=jnp.int32)
    return drawn.at[0, N_CTX - 1].set(N_CTX - 1)


def shard_levels(rng, extent, pieces, low, largest):
    loudness, own = 1.0, jax.random.fold_in(rng, 6)
    for dim, parts in pieces:
        steps = jnp.exp(jax.random.uniform(jax.random.fold_in(own, dim), (parts,), jnp.float32, low / len(pieces), largest / len(pieces)))
        loudness = loudness * jnp.repeat(steps, extent[dim] // parts).reshape([-1 if axis == dim else 1 for axis in range(len(extent))])
    return loudness


def length_profile(amount, total, limit, skew):
    loads = [(1 << 20) // math.isqrt(standing ** skew) + 1 for standing in range(2, amount + 1)]
    spare, counts = total - limit - (amount - 1), [1] * (amount - 1)
    while spare > 0:
        movable = [i for i in range(amount - 1) if counts[i] < limit]
        mass, left = sum([loads[i] for i in movable]), spare
        for i in movable:
            more = min(limit - counts[i], max(1, left * loads[i] // mass), spare)
            counts[i] = counts[i] + more
            spare = spare - more
    return np.array([limit] + counts)


def uneven(key, number_of, total, reach, lean):
    if number_of == 2:
        one = jax.random.randint(key, (), max(1, total - reach), min(reach, total - 1) + 1)
        return jnp.stack([one, total - one])
    sizes = jnp.asarray(length_profile(number_of, total, reach, lean), jnp.int32)
    pairs = (number_of - 1) // 2
    donor, sink = sizes[1:1 + 2 * pairs:2], sizes[2:2 + 2 * pairs:2]
    room = jnp.minimum(donor - 1, reach - sink)
    passed = jax.random.randint(jax.random.fold_in(key, 1), (pairs,), 0, 1 << 20) % (room + 1)
    sizes = sizes.at[1:1 + 2 * pairs:2].set(donor - passed).at[2:2 + 2 * pairs:2].set(sink + passed)
    return sizes[jax.random.permutation(jax.random.fold_in(key, 2), number_of)]


def centred(key, extent, width, most, cuts=(), kind=jnp.bfloat16):
    result = width * jax.random.normal(key, extent, jnp.float32)
    if cuts:
        result = result * shard_levels(key, extent, cuts, -0.22, 0.18)
    return jnp.clip(result, -most, most).astype(kind)


def setup_inputs(seed: int = 0, part: int = 0) -> dict:
    seeds = jax.random.split(jax.random.key(seed), 8)
    part_splits = jax.random.split(jax.random.fold_in(seeds[7], part), 8)
    return {
        "queries": draw_queries(jax.random.fold_in(jax.random.fold_in(seeds[7], part), 71), part),
        "keys": draw_keys(jax.random.fold_in(jax.random.fold_in(seeds[7], part), 71), part),
        "values": centred(part_splits[2], (DOC_COUNT, DOC_TOKENS, KEY_VALUE_HEADS * HEAD_SIZE), 1.0, 6.0, ((0, 2), (1, 4), (2, 2))),
        "tok_ids": jax.vmap(lambda own: jnp.searchsorted(jnp.cumsum(uneven(own, 4 * N_CTX, DOC_TOKENS, SEGMENT_TOKENS // 2, 1)), jnp.arange(DOC_TOKENS), side="right"))(jax.random.split(part_splits[3], DOC_COUNT)).reshape((DOC_COUNT, DOC_TOKENS)).astype(jnp.int32),
        "vis_start": draw_vis_start(jax.random.fold_in(jax.random.fold_in(seeds[7], part), 71), part),
        "out_weight": centred(seeds[5], (D, QUERY_HEADS * HEAD_SIZE), (QUERY_HEADS * HEAD_SIZE) ** -0.5, 0.125, ((0, 2), (1, 2))),
        "grad_out": centred(part_splits[6], (DOC_COUNT, DOC_TOKENS, D), 1.0, 6.0, ((0, 2), (1, 4))),
    }


NEG_FILL = -1e30


def round_keep(value):
    narrow = value.astype(jnp.bfloat16)
    narrow = lax.optimization_barrier(narrow)
    return narrow.astype(jnp.float32)


def segment_backward(segment_queries, segment_key_rows, segment_value_rows, allowed, segment_output_gradient):
    head_groups = QUERY_HEADS // KEY_VALUE_HEADS
    row_block = segment_queries.shape[0]
    column_width = segment_key_rows.shape[0]
    scale = HEAD_SIZE ** -0.5
    query_head_count = segment_queries.astype(jnp.float32).reshape(row_block, KEY_VALUE_HEADS, head_groups, HEAD_SIZE)
    key_head_count = segment_key_rows.astype(jnp.float32).reshape(column_width, KEY_VALUE_HEADS, HEAD_SIZE)
    value_head_count = segment_value_rows.astype(jnp.float32).reshape(column_width, KEY_VALUE_HEADS, HEAD_SIZE)
    head_dimension = segment_output_gradient.astype(jnp.float32).reshape(row_block, KEY_VALUE_HEADS, head_groups, HEAD_SIZE)
    scores = jnp.einsum('shgd,khd->hgsk', query_head_count, key_head_count) * scale
    scores = jnp.where(allowed[None, None], scores, NEG_FILL)
    top = jnp.max(scores, axis=-1, keepdims=True)
    expo = jnp.exp(scores - top)
    prob = expo / jnp.sum(expo, axis=-1, keepdims=True)
    probs_b = round_keep(prob)
    attn = jnp.einsum('hgsk,khd->shgd', probs_b, value_head_count).astype(jnp.bfloat16)
    delta = jnp.sum(head_dimension * attn.astype(jnp.float32), axis=-1)
    dprob = jnp.einsum('shgd,khd->hgsk', head_dimension, value_head_count)
    dscore = prob * (dprob - jnp.transpose(delta, (1, 2, 0))[..., None])
    ds_b = round_keep(dscore)
    grad_q = (scale * jnp.einsum('hgsk,khd->shgd', ds_b, key_head_count)).astype(jnp.bfloat16)
    key_gradient = scale * jnp.einsum('hgsk,shgd->khd', ds_b, query_head_count)
    value_gradient = jnp.einsum('hgsk,shgd->khd', probs_b, head_dimension)
    return (attn.reshape(row_block, QUERY_HEADS * HEAD_SIZE), grad_q.reshape(row_block, QUERY_HEADS * HEAD_SIZE),
            key_gradient.reshape(column_width, KEY_VALUE_HEADS * HEAD_SIZE), value_gradient.reshape(column_width, KEY_VALUE_HEADS * HEAD_SIZE))


def reference(queries, keys, values, tok_ids, vis_start, out_weight, grad_out):
    flat_out = grad_out.reshape(DOC_COUNT * DOC_TOKENS, D)
    d_attn = jnp.dot(flat_out, out_weight, preferred_element_type=jnp.float32).astype(jnp.bfloat16)
    d_attn = d_attn.reshape(DOC_COUNT, N_CTX, SEGMENT_TOKENS, QUERY_HEADS * HEAD_SIZE)
    positions = jnp.arange(SEGMENT_TOKENS, dtype=jnp.int32)
    causal = positions[:, None] >= positions[None, :]
    summ_seg = jnp.arange(N_CTX * SUMMARY_TOKENS, dtype=jnp.int32) // SUMMARY_TOKENS
    attn_list, gq_list, key_gradient_list, value_gradient_list = [], [], [], []
    for doc_index in range(DOC_COUNT):
        q_doc = queries[doc_index].reshape(N_CTX, SEGMENT_TOKENS, QUERY_HEADS * HEAD_SIZE)
        document_keys = keys[doc_index].reshape(N_CTX, SEGMENT_TOKENS, KEY_VALUE_HEADS * HEAD_SIZE)
        document_values = values[doc_index].reshape(N_CTX, SEGMENT_TOKENS, KEY_VALUE_HEADS * HEAD_SIZE)
        ids_doc = tok_ids[doc_index].reshape(N_CTX, SEGMENT_TOKENS)
        summary_key_rows = document_keys[:, SEGMENT_TOKENS - SUMMARY_TOKENS:].reshape(N_CTX * SUMMARY_TOKENS, KEY_VALUE_HEADS * HEAD_SIZE)
        summary_value_rows = document_values[:, SEGMENT_TOKENS - SUMMARY_TOKENS:].reshape(N_CTX * SUMMARY_TOKENS, KEY_VALUE_HEADS * HEAD_SIZE)

        def step(carry, inputs):
            segment_queries, seg_k, seg_v, seg_ids, segment_output_gradient, start, place = inputs
            own = causal & (seg_ids[:, None] == seg_ids[None, :])
            seen = (summ_seg >= start) & (summ_seg < place)
            allowed = jnp.concatenate([own, jnp.broadcast_to(seen[None, :], (SEGMENT_TOKENS, N_CTX * SUMMARY_TOKENS))], axis=1)
            attn, grad_q, key_gradient, value_gradient = segment_backward(
                segment_queries, jnp.concatenate([seg_k, summary_key_rows], 0), jnp.concatenate([seg_v, summary_value_rows], 0), allowed, segment_output_gradient)
            carry = (carry[0] + key_gradient[SEGMENT_TOKENS:], carry[1] + value_gradient[SEGMENT_TOKENS:])
            return carry, (attn, grad_q, key_gradient[:SEGMENT_TOKENS], value_gradient[:SEGMENT_TOKENS])

        empty_block = jnp.zeros((N_CTX * SUMMARY_TOKENS, KEY_VALUE_HEADS * HEAD_SIZE), jnp.float32)
        places = jnp.arange(N_CTX, dtype=jnp.int32)
        partial_sums, outs = lax.scan(step, (empty_block, empty_block),
                              (q_doc, document_keys, document_values, ids_doc, d_attn[doc_index], vis_start[doc_index], places))
        attn, grad_q, key_gradient, value_gradient = outs
        key_gradient = key_gradient.at[:, SEGMENT_TOKENS - SUMMARY_TOKENS:].add(partial_sums[0].reshape(N_CTX, SUMMARY_TOKENS, KEY_VALUE_HEADS * HEAD_SIZE))
        value_gradient = value_gradient.at[:, SEGMENT_TOKENS - SUMMARY_TOKENS:].add(partial_sums[1].reshape(N_CTX, SUMMARY_TOKENS, KEY_VALUE_HEADS * HEAD_SIZE))
        attn_list.append(attn.reshape(DOC_TOKENS, QUERY_HEADS * HEAD_SIZE))
        gq_list.append(grad_q.reshape(DOC_TOKENS, QUERY_HEADS * HEAD_SIZE))
        key_gradient_list.append(key_gradient.astype(jnp.bfloat16).reshape(DOC_TOKENS, KEY_VALUE_HEADS * HEAD_SIZE))
        value_gradient_list.append(value_gradient.astype(jnp.bfloat16).reshape(DOC_TOKENS, KEY_VALUE_HEADS * HEAD_SIZE))
    attn_all = jnp.stack(attn_list).reshape(DOC_COUNT * DOC_TOKENS, QUERY_HEADS * HEAD_SIZE)
    weight_grad = jnp.dot(flat_out.T, attn_all, preferred_element_type=jnp.float32).astype(jnp.bfloat16)
    return jnp.stack(gq_list), jnp.stack(key_gradient_list), jnp.stack(value_gradient_list), weight_grad
```

```python
import functools

import jax
import jax.numpy as jnp
from jax import lax
from jax.experimental import pallas as pl
from jax.experimental.pallas import tpu as pltpu
from jax.sharding import PartitionSpec as P

HEAD_SIZE = 128
SUMMARY_TOKENS = 64
SCALE = HEAD_SIZE ** (-0.5)
NEG_FILL = -1e30
VMEM_LIMIT = 48 * 1024 * 1024

VMEM = pltpu.MemorySpace.VMEM
SMEM = pltpu.MemorySpace.SMEM


def dot(a, b, contract):
    return lax.dot_general(a, b, (contract, ((), ())), preferred_element_type=jnp.float32)


def mask_bias(count_ref, id_column_ref, id_row_ref, shape, seg_len):
    rows = lax.broadcasted_iota(jnp.int32, shape, 0)
    cols = lax.broadcasted_iota(jnp.int32, shape, 1)
    own = (rows >= cols) & (id_column_ref[...] == id_row_ref[...])
    far = (cols >= seg_len) & (cols < seg_len + SUMMARY_TOKENS * count_ref[0, 0])
    return jnp.where(own | far, 0.0, NEG_FILL).astype(jnp.float32)


def softmax_rows(q_head, k_head, bias):
    scores = dot(q_head, k_head, ((1,), (1,))) * SCALE + bias
    top = jnp.max(scores, axis=-1, keepdims=True)
    expo = jnp.exp(scores - top)
    return expo / jnp.sum(expo, axis=-1, keepdims=True)


def forward_kernel(count_ref, idc_ref, idr_ref, q_ref, k_ref, v_ref, attn_ref, bias_ref):
    seg_len, q_width = q_ref.shape
    kv_heads = k_ref.shape[1] // HEAD_SIZE
    group = q_width // k_ref.shape[1]
    bias_ref[...] = mask_bias(count_ref, idc_ref, idr_ref, bias_ref.shape, seg_len)
    for kv in range(kv_heads):
        kv_cols = slice(kv * HEAD_SIZE, (kv + 1) * HEAD_SIZE)
        for g in range(group):
            h = kv * group + g
            cols = slice(h * HEAD_SIZE, (h + 1) * HEAD_SIZE)
            probs_b = softmax_rows(q_ref[:, cols], k_ref[:, kv_cols], bias_ref[...]).astype(jnp.bfloat16)
            attn_ref[:, cols] = dot(probs_b, v_ref[:, kv_cols], ((1,), (0,))).astype(jnp.bfloat16)


def backward_kernel(count_ref, idc_ref, idr_ref, q_ref, k_ref, v_ref, attn_ref, d_mine_ref, d_part_ref,
                    gq_ref, gkv_ref, bias_ref):
    seg_len, q_width = q_ref.shape
    kv_width = k_ref.shape[1]
    kv_heads = kv_width // HEAD_SIZE
    group = q_width // kv_width
    bias_ref[...] = mask_bias(count_ref, idc_ref, idr_ref, bias_ref.shape, seg_len)
    for kv in range(kv_heads):
        kv_cols = slice(kv * HEAD_SIZE, (kv + 1) * HEAD_SIZE)
        k_head = k_ref[:, kv_cols]
        v_head = v_ref[:, kv_cols]
        grad_k = jnp.zeros((k_ref.shape[0], HEAD_SIZE), jnp.float32)
        grad_v = jnp.zeros((k_ref.shape[0], HEAD_SIZE), jnp.float32)
        for g in range(group):
            h = kv * group + g
            cols = slice(h * HEAD_SIZE, (h + 1) * HEAD_SIZE)
            q_head = q_ref[:, cols]
            d_sum = d_mine_ref[:, cols]
            for part in range(d_part_ref.shape[0]):
                d_sum = d_sum + d_part_ref[part, :, cols].astype(jnp.float32)
            d_head = d_sum.astype(jnp.bfloat16)
            prob = softmax_rows(q_head, k_head, bias_ref[...])
            probs_b = prob.astype(jnp.bfloat16)
            delta = jnp.sum(
                d_head.astype(jnp.float32) * attn_ref[:, cols].astype(jnp.float32), axis=-1, keepdims=True
            )
            dprob = dot(d_head, v_head, ((1,), (1,)))
            ds_b = (prob * (dprob - delta)).astype(jnp.bfloat16)
            gq_ref[:, cols] = (SCALE * dot(ds_b, k_head, ((1,), (0,)))).astype(jnp.bfloat16)
            grad_k += dot(ds_b, q_head, ((0,), (0,)))
            grad_v += dot(probs_b, d_head, ((0,), (0,)))
        gkv_ref[:, kv_cols] = SCALE * grad_k
        gkv_ref[:, kv_width + kv * HEAD_SIZE : kv_width + (kv + 1) * HEAD_SIZE] = grad_v


def call_attention(kernel, out_shape, operands, bias_shape, flops):
    return pl.pallas_call(
        kernel,
        out_shape=out_shape,
        in_specs=[pl.BlockSpec(memory_space=SMEM)] + [pl.BlockSpec(memory_space=VMEM)] * (len(operands) - 1),
        out_specs=jax.tree.map(lambda _: pl.BlockSpec(memory_space=VMEM), out_shape),
        scratch_shapes=[pltpu.VMEM(bias_shape, jnp.float32)],
        compiler_params=pltpu.CompilerParams(vmem_limit_bytes=VMEM_LIMIT),
        cost_estimate=pl.CostEstimate(flops=flops, bytes_accessed=4 << 20, transcendentals=1 << 20),
    )(*operands)


def weight_kernel(blocks, has_acc, info_ref, *refs):
    ins, out_ref = refs[:-1], refs[-1]
    acc_ref = None
    if has_acc:
        acc_ref, ins = ins[0], ins[1:]
    core = info_ref[0]
    total = jnp.zeros(out_ref.shape, jnp.float32) if acc_ref is None else acc_ref[...]
    at = 0
    for whole in blocks:
        if whole:
            rows = ins[at][...]
            attn = ins[at + 1][...]
            at += 2
        else:
            mine, other, attn = ins[at][...], ins[at + 1][...], ins[at + 2][...]
            low = jnp.where(core == 0, mine, other)
            high = jnp.where(core == 0, other, mine)
            rows = jnp.concatenate([low, high], 0)
            at += 3
        total += dot(rows, attn, ((0,), (0,)))
    out_ref[...] = total.astype(out_ref.dtype)


def weight_stage(info, acc, blocks, out_dtype, tile):
    operands = [] if acc is None else [acc]
    width = blocks[0][-1].shape[1]
    height = blocks[0][0].shape[1]
    in_specs = [] if acc is None else [pl.BlockSpec((tile, width), lambda i, s: (i, 0))]
    flops = 0
    moved = (0 if acc is None else acc.size * 4) + height * width * jnp.dtype(out_dtype).itemsize
    for block in blocks:
        for part in block[:-1]:
            operands.append(part)
            in_specs.append(pl.BlockSpec((part.shape[0], tile), lambda i, s: (0, i)))
            moved += part.size * 2
        operands.append(block[-1])
        in_specs.append(pl.BlockSpec(block[-1].shape, lambda i, s: (0, 0)))
        flops += 2 * block[-1].size * height
        moved += block[-1].size * 2
    return pl.pallas_call(
        functools.partial(weight_kernel, [len(b) == 2 for b in blocks], acc is not None),
        out_shape=jax.ShapeDtypeStruct((height, width), out_dtype),
        grid_spec=pltpu.PrefetchScalarGridSpec(
            num_scalar_prefetch=1,
            grid=(height // tile,),
            in_specs=in_specs,
            out_specs=pl.BlockSpec((tile, width), lambda i, s: (i, 0)),
        ),
        compiler_params=pltpu.CompilerParams(vmem_limit_bytes=VMEM_LIMIT),
        cost_estimate=pl.CostEstimate(flops=flops, bytes_accessed=moved, transcendentals=0),
    )(info, *operands)


def turn(x, axis, step):
    n = lax.axis_size(axis)
    return lax.ppermute(x, axis, [(i, (i + step) % n) for i in range(n)])


def line_pairs(n, step):
    return [(i, i + step) for i in range(n) if 0 <= i + step < n]


def spread(x):
    right = lax.ppermute(x, "ctx", line_pairs(4, 1))
    left = lax.ppermute(x, "ctx", line_pairs(4, -1))
    two = lax.ppermute(x, "ctx", [(0, 2), (1, 3), (2, 0), (3, 1)])
    three = lax.ppermute(two, "ctx", [(1, 0), (2, 3)])
    return [right, left, two, three]


def after(x, *others):
    return lax.optimization_barrier((x, *others))[0]


def shards(queries, keys, values, tok_ids, vis_start, out_weight, grad_out):
    seg_len = queries.shape[1]
    kv_width = keys.shape[2]
    d_model = grad_out.shape[2]
    part_rows = out_weight.shape[0]
    n_ctx = lax.axis_size("ctx")
    n_dp = lax.axis_size("dp")
    n_head = lax.axis_size("head")
    place = lax.axis_index("ctx")
    me_dp = lax.axis_index("dp")
    me_head = lax.axis_index("head")
    half = seg_len // n_head
    cut = seg_len - SUMMARY_TOKENS

    tail = jnp.concatenate([keys[0, cut:], values[0, cut:]], axis=1)
    far = [lax.ppermute(tail, "ctx", line_pairs(n_ctx, s)) for s in range(1, n_ctx)]
    far_len = -(-(n_ctx - 1) * SUMMARY_TOKENS // HEAD_SIZE) * HEAD_SIZE
    far.append(jnp.zeros((far_len - (n_ctx - 1) * SUMMARY_TOKENS, 2 * kv_width), keys.dtype))
    far = jnp.concatenate(far, axis=0)
    all_keys = jnp.concatenate([keys[0], far[:, :kv_width]], axis=0)
    all_vals = jnp.concatenate([values[0], far[:, kv_width:]], axis=0)
    n_keys = seg_len + far_len

    rows_half = lax.dynamic_slice(grad_out[0], (me_head * half, 0), (half, d_model))
    own_rows = lax.dynamic_slice(grad_out[0], (0, me_dp * part_rows), (seg_len, part_rows))
    own_half = lax.dynamic_slice(rows_half, (0, me_dp * part_rows), (half, part_rows))
    peer_half = []
    for s in range(1, n_dp):
        to = lax.rem(me_dp + s, n_dp)
        peer_half.append(turn(lax.dynamic_slice(rows_half, (0, to * part_rows), (half, part_rows)), "dp", s))
    peer_other = [turn(x, "head", 1) for x in peer_half]

    wide = n_ctx != 4
    if not wide:
        own_z = spread(own_half)

    count = (place - vis_start[0, 0]).reshape(1, 1).astype(jnp.int32)
    id_column = tok_ids[0].reshape(seg_len, 1)
    id_row = jnp.pad(tok_ids, ((0, 0), (0, far_len)), constant_values=-1)
    pair_flops = 2 * seg_len * n_keys * queries.shape[2]
    attn = call_attention(
        forward_kernel,
        jax.ShapeDtypeStruct(queries.shape[1:], jnp.bfloat16),
        (count, id_column, id_row, queries[0], all_keys, all_vals),
        (seg_len, n_keys),
        2 * pair_flops,
    )
    if not wide:
        attn_z = [attn] + spread(attn)
        attn_x = []
        for s in range(1, n_dp):
            attn_x.append([turn(x, "dp", s) for x in attn_z])

    first_core = me_head == 0
    back = []
    for s in range(1, n_dp):
        mine, other = peer_half[s - 1], peer_other[s - 1]
        rows = jnp.concatenate([jnp.where(first_core, mine, other), jnp.where(first_core, other, mine)], 0)
        part = jnp.dot(rows, out_weight, preferred_element_type=jnp.float32).astype(jnp.bfloat16)
        back.append(turn(part, "dp", -s))
    d_mine = jnp.dot(own_rows, out_weight, preferred_element_type=jnp.float32)
    d_part = jnp.stack(back)

    grad_q, grad_kv = call_attention(
        backward_kernel,
        (
            jax.ShapeDtypeStruct(queries.shape[1:], jnp.bfloat16),
            jax.ShapeDtypeStruct((n_keys, 2 * kv_width), jnp.float32),
        ),
        (count, id_column, id_row, queries[0], all_keys, all_vals, attn, d_mine, d_part),
        (seg_len, n_keys),
        5 * pair_flops,
    )
    home = grad_kv[cut:seg_len]
    for s in range(1, n_ctx):
        begin = seg_len + (s - 1) * SUMMARY_TOKENS
        home = home + lax.ppermute(grad_kv[begin : begin + SUMMARY_TOKENS], "ctx", line_pairs(n_ctx, -s))
    out_kv = jnp.concatenate([grad_kv[:cut], home], 0).astype(jnp.bfloat16)
    out_k, out_v = out_kv[:, :kv_width], out_kv[:, kv_width:]

    if wide:
        block = d_model // (n_ctx * n_dp)
        columns = (
            grad_out[0].reshape(seg_len, n_dp, n_ctx, block).transpose(0, 2, 1, 3).reshape(seg_len, d_model)
        )
        shard = lax.psum_scatter(
            jnp.einsum("sd,se->de", columns, attn, preferred_element_type=jnp.float32),
            ("ctx", "dp"),
            scatter_dimension=0,
            tiled=True,
        ).astype(jnp.bfloat16)
        weight_grad = lax.all_gather(shard, "ctx", axis=0, tiled=True)
    else:
        info = me_head.reshape(1).astype(jnp.int32)
        own_other = [turn(x, "head", 1) for x in own_z]
        acc = weight_stage(
            info,
            None,
            [(own_rows, attn)] + list(zip(own_z, own_other, attn_z[1:])),
            jnp.float32,
            256,
        )
        for s in range(1, n_dp):
            start = after(peer_half[s - 1], *own_z)
            peer_z = spread(start)
            other_z = [turn(x, "head", 1) for x in peer_z]
            acc = weight_stage(
                info,
                acc,
                list(zip([start] + peer_z, [peer_other[s - 1]] + other_z, attn_x[s - 1])),
                jnp.bfloat16 if s == n_dp - 1 else jnp.float32,
                256,
            )
        weight_grad = acc
    return (grad_q[None], out_k[None], out_v[None], weight_grad)


def solution(mesh):
    placed = (
        P(("groups", "dp"), "ctx", "head"),
        P(("groups", "dp"), "ctx", "head"),
        P(("groups", "dp"), "ctx", "head"),
        P(("groups", "dp"), "ctx"),
        P(("groups", "dp"), "ctx"),
        P("dp", "head"),
        P(("groups", "dp"), "ctx", None),
    )
    return jax.shard_map(
        shards,
        mesh=mesh,
        in_specs=placed,
        out_specs=(
            P(("groups", "dp"), "ctx", "head"),
            P(("groups", "dp"), "ctx", "head"),
            P(("groups", "dp"), "ctx", "head"),
            P(("groups", "dp"), "head"),
        ),
        check_vma=False,
    )
```

```python
import functools

import jax
import jax.numpy as jnp
from jax import lax
from jax.experimental import pallas as pl
from jax.experimental.pallas import tpu as pltpu
from jax.sharding import PartitionSpec as P

HEAD_SIZE = 128
SUMMARY_TOKENS = 64
SCALE = HEAD_SIZE ** (-0.5)
NEG_FILL = -1e30
MARK = 20_000_000_000
VMEM_LIMIT = 48 * 1024 * 1024

VMEM = pltpu.MemorySpace.VMEM
SMEM = pltpu.MemorySpace.SMEM


def dot(a, b, contract):
    return lax.dot_general(a, b, (contract, ((), ())), preferred_element_type=jnp.float32)


def mask_bias(count_ref, id_column_ref, id_row_ref, shape, seg_len):
    rows = lax.broadcasted_iota(jnp.int32, shape, 0)
    cols = lax.broadcasted_iota(jnp.int32, shape, 1)
    own = (rows >= cols) & (id_column_ref[...] == id_row_ref[...])
    far = (cols >= seg_len) & (cols < seg_len + SUMMARY_TOKENS * count_ref[0, 0])
    return jnp.where(own | far, 0.0, NEG_FILL).astype(jnp.float32)


def softmax_rows(q_head, k_head, bias):
    scores = dot(q_head, k_head, ((1,), (1,))) * SCALE + bias
    top = jnp.max(scores, axis=-1, keepdims=True)
    expo = jnp.exp(scores - top)
    return expo / jnp.sum(expo, axis=-1, keepdims=True)


def forward_kernel(n_head, count_ref, idc_ref, idr_ref, q_ref, k_ref, v_ref, attn_ref, turned_ref, bias_ref):
    seg_len, q_width = q_ref.shape
    kv_heads = k_ref.shape[1] // HEAD_SIZE
    group = q_width // k_ref.shape[1]
    share = seg_len // n_head
    bias_ref[...] = mask_bias(count_ref, idc_ref, idr_ref, bias_ref.shape, seg_len)
    for kv in range(kv_heads):
        kv_cols = slice(kv * HEAD_SIZE, (kv + 1) * HEAD_SIZE)
        for g in range(group):
            h = kv * group + g
            cols = slice(h * HEAD_SIZE, (h + 1) * HEAD_SIZE)
            probs_b = softmax_rows(q_ref[:, cols], k_ref[:, kv_cols], bias_ref[...]).astype(jnp.bfloat16)
            attn = dot(probs_b, v_ref[:, kv_cols], ((1,), (0,))).astype(jnp.bfloat16)
            attn_ref[:, cols] = attn
            for core in range(n_head):
                to = lax.rem(core + n_head - count_ref[0, 1], n_head) * share
                turned_ref[pl.ds(pl.multiple_of(to, share), share), cols] = attn[core * share : (core + 1) * share]


def backward_kernel(count_ref, idc_ref, idr_ref, q_ref, k_ref, v_ref, attn_ref, d_mine_ref, d_part_ref, token_ref,
                    gq_ref, gkv_ref, bias_ref):
    seg_len, q_width = q_ref.shape
    kv_width = k_ref.shape[1]
    kv_heads = kv_width // HEAD_SIZE
    group = q_width // kv_width
    bias_ref[...] = mask_bias(count_ref, idc_ref, idr_ref, bias_ref.shape, seg_len)
    for kv in range(kv_heads):
        kv_cols = slice(kv * HEAD_SIZE, (kv + 1) * HEAD_SIZE)
        k_head = k_ref[:, kv_cols]
        v_head = v_ref[:, kv_cols]
        grad_k = jnp.zeros((k_ref.shape[0], HEAD_SIZE), jnp.float32)
        grad_v = jnp.zeros((k_ref.shape[0], HEAD_SIZE), jnp.float32)
        for g in range(group):
            h = kv * group + g
            cols = slice(h * HEAD_SIZE, (h + 1) * HEAD_SIZE)
            q_head = q_ref[:, cols]
            d_sum = d_mine_ref[:, cols]
            for part in range(d_part_ref.shape[0]):
                d_sum = d_sum + d_part_ref[part, :, cols].astype(jnp.float32)
            d_head = d_sum.astype(jnp.bfloat16)
            prob = softmax_rows(q_head, k_head, bias_ref[...])
            probs_b = prob.astype(jnp.bfloat16)
            delta = jnp.sum(
                d_head.astype(jnp.float32) * attn_ref[:, cols].astype(jnp.float32), axis=-1, keepdims=True
            )
            dprob = dot(d_head, v_head, ((1,), (1,)))
            ds_b = (prob * (dprob - delta)).astype(jnp.bfloat16)
            gq_ref[:, cols] = (SCALE * dot(ds_b, k_head, ((1,), (0,)))).astype(jnp.bfloat16)
            grad_k += dot(ds_b, q_head, ((0,), (0,)))
            grad_v += dot(probs_b, d_head, ((0,), (0,)))
        gkv_ref[:, kv_cols] = SCALE * grad_k
        gkv_ref[:, kv_width + kv * HEAD_SIZE : kv_width + (kv + 1) * HEAD_SIZE] = grad_v


def call_attention(kernel, out_shape, operands, bias_shape, flops):
    return pl.pallas_call(
        kernel,
        out_shape=out_shape,
        in_specs=[pl.BlockSpec(memory_space=SMEM)] + [pl.BlockSpec(memory_space=VMEM)] * (len(operands) - 1),
        out_specs=jax.tree.map(lambda _: pl.BlockSpec(memory_space=VMEM), out_shape),
        scratch_shapes=[pltpu.VMEM(bias_shape, jnp.float32)],
        compiler_params=pltpu.CompilerParams(vmem_limit_bytes=VMEM_LIMIT),
        cost_estimate=pl.CostEstimate(flops=flops, bytes_accessed=4 << 20, transcendentals=1 << 20),
    )(*operands)


def mark_kernel(*refs):
    refs[-1][...] = refs[0][...]


def mark(token, *done):
    return pl.pallas_call(
        mark_kernel,
        out_shape=jax.ShapeDtypeStruct(token.shape, token.dtype),
        in_specs=[pl.BlockSpec(memory_space=VMEM)] + [pl.BlockSpec(memory_space=pl.ANY)] * len(done),
        out_specs=pl.BlockSpec(memory_space=VMEM),
        cost_estimate=pl.CostEstimate(flops=MARK, bytes_accessed=0, transcendentals=0),
    )(token, *done)


def outer(rows, attn):
    contract = tuple(range(rows.ndim - 1))
    return dot(rows, attn, (contract, contract))


def turn(x, axis, step, name):
    n = lax.axis_size(axis)
    with jax.named_scope(name):
        return lax.ppermute(x, axis, [(i, (i + step) % n) for i in range(n)])


def line_pairs(n, step):
    return [(i, i + step) for i in range(n) if 0 <= i + step < n]


def pairs(x, name):
    with jax.named_scope(name + "_pairs"):
        return lax.ppermute(x, "ctx", [(0, 1), (1, 0), (2, 3), (3, 2)])


def middle(x, name):
    with jax.named_scope(name + "_middle"):
        return lax.ppermute(x, "ctx", [(1, 2), (2, 1)])


def two_away(x, name):
    with jax.named_scope(name + "_two"):
        return lax.ppermute(x, "ctx", [(0, 2), (1, 3), (2, 0), (3, 1)])


def ends(x, name):
    with jax.named_scope(name + "_ends"):
        return lax.ppermute(x, "ctx", [(1, 0), (2, 3)])


def gate(arrays, *done):
    out = lax.optimization_barrier((*arrays, *done))
    return list(out[: len(arrays)]), list(out[len(arrays) :])


def shards(queries, keys, values, tok_ids, vis_start, out_weight, grad_out):
    seg_len = queries.shape[1]
    kv_width = keys.shape[2]
    d_model = grad_out.shape[2]
    part_rows = out_weight.shape[0]
    n_ctx = lax.axis_size("ctx")
    n_dp = lax.axis_size("dp")
    n_head = lax.axis_size("head")
    place = lax.axis_index("ctx")
    me_dp = lax.axis_index("dp")
    me_head = lax.axis_index("head")
    half = seg_len // n_head
    cut = seg_len - SUMMARY_TOKENS

    tail = jnp.concatenate([keys[0, cut:], values[0, cut:]], axis=1)
    far = [lax.ppermute(tail, "ctx", line_pairs(n_ctx, s)) for s in range(1, n_ctx)]
    far_len = -(-(n_ctx - 1) * SUMMARY_TOKENS // HEAD_SIZE) * HEAD_SIZE
    far.append(jnp.zeros((far_len - (n_ctx - 1) * SUMMARY_TOKENS, 2 * kv_width), keys.dtype))
    far = jnp.concatenate(far, axis=0)
    all_keys = jnp.concatenate([keys[0], far[:, :kv_width]], axis=0)
    all_vals = jnp.concatenate([values[0], far[:, kv_width:]], axis=0)
    n_keys = seg_len + far_len

    wide = n_ctx != 4
    token = jnp.zeros((8, 128), jnp.float32)

    def rows_of(core, dp):
        return lax.dynamic_slice(grad_out[0], (core * half, dp * part_rows), (half, part_rows))

    own = rows_of(me_head, me_dp)
    peer, peer_other = [], []
    for s in range(1, n_dp):
        to = lax.rem(me_dp + s, n_dp)
        peer.append(turn(rows_of(me_head, to), "dp", s, "peer_in"))

    count = jnp.stack([place - vis_start[0, 0], me_head]).reshape(1, 2).astype(jnp.int32)
    id_column = tok_ids[0].reshape(seg_len, 1)
    id_row = jnp.pad(tok_ids, ((0, 0), (0, far_len)), constant_values=-1)
    pair_flops = 2 * seg_len * n_keys * queries.shape[2]
    attn, turned = call_attention(
        functools.partial(forward_kernel, n_head),
        (jax.ShapeDtypeStruct(queries.shape[1:], jnp.bfloat16),) * 2,
        (count, id_column, id_row, queries[0], all_keys, all_vals),
        (seg_len, n_keys),
        2 * pair_flops,
    )

    peer, (attn,) = gate(peer, attn)
    peer_other = [turn(x, "head", 1, "peer_s") for x in peer]
    first_core = me_head == 0
    parts = []
    for s in range(1, n_dp):
        mine, other = peer[s - 1], peer_other[s - 1]
        rows = jnp.concatenate([jnp.where(first_core, mine, other), jnp.where(first_core, other, mine)], 0)
        parts.append(jnp.dot(rows, out_weight, preferred_element_type=jnp.float32).astype(jnp.bfloat16))
    back = [turn(part, "dp", -s, "back") for s, part in zip(range(1, n_dp), parts)]
    own_rows = lax.dynamic_slice(grad_out[0], (0, me_dp * part_rows), (seg_len, part_rows))
    d_mine = jnp.dot(own_rows, out_weight, preferred_element_type=jnp.float32)
    d_part = jnp.stack(back)

    def backward(d_part):
        return call_attention(
            backward_kernel,
            (
                jax.ShapeDtypeStruct(queries.shape[1:], jnp.bfloat16),
                jax.ShapeDtypeStruct((n_keys, 2 * kv_width), jnp.float32),
            ),
            (count, id_column, id_row, queries[0], all_keys, all_vals, attn, d_mine, d_part, token),
            (seg_len, n_keys),
            5 * pair_flops,
        )


    def send_home(grad_kv):
        sent = []
        for s in range(1, n_ctx):
            begin = seg_len + (s - 1) * SUMMARY_TOKENS
            with jax.named_scope("grads"):
                sent.append(lax.ppermute(grad_kv[begin : begin + SUMMARY_TOKENS], "ctx", line_pairs(n_ctx, -s)))
        return sent

    def add_home(grad_kv, sent):
        home = sum(sent, grad_kv[cut:seg_len])
        return jnp.concatenate([grad_kv[:cut], home], 0).astype(jnp.bfloat16)

    if wide:
        grad_q, grad_kv = backward(d_part)
        out_kv = add_home(grad_kv, send_home(grad_kv))
        block = d_model // (n_ctx * n_dp)
        columns = (
            grad_out[0].reshape(seg_len, n_dp, n_ctx, block).transpose(0, 2, 1, 3).reshape(seg_len, d_model)
        )
        shard = lax.psum_scatter(
            jnp.einsum("sd,se->de", columns, attn, preferred_element_type=jnp.float32),
            ("ctx", "dp"),
            scatter_dimension=0,
            tiled=True,
        ).astype(jnp.bfloat16)
        weight_grad = lax.all_gather(shard, "ctx", axis=0, tiled=True)
    else:
        steps = range(1, n_dp)
        at_end = (place == 0) | (place == n_ctx - 1)

        def swap(x, name):
            return turn(x, "head", 1, name)

        own_1 = pairs(own, "own")
        own_2 = two_away(own, "own")
        own_mid = middle(own, "own")
        attn_1 = pairs(turned, "attn")
        attn_x0 = [turn(turned, "dp", s, "attn_x0") for s in steps]
        token = mark(token, own_1, own_2, own_mid)
        (attn_0, own_2, *peer), (token,) = gate([turned, own_2, *peer], token)
        own_end = ends(own_2, "own")
        peer_1 = [pairs(x, "peer") for x in peer]
        attn_mid_a = middle(attn_0, "attn_a")
        token = mark(token)
        (attn_1,), (token,) = gate([attn_1], token)
        attn_mid_b = middle(attn_1, "attn_b")
        attn_end_a = ends(attn_mid_a, "attn_a")
        attn_x1 = [turn(attn_1, "dp", s, "attn_x1") for s in steps]
        peer_pair = [jnp.stack([a, b]) for a, b in zip(peer, peer_1)]
        peer_pair, (attn_mid_b, own_end, d_part) = gate(peer_pair, attn_mid_b, own_end, d_part)
        attn_end_b = ends(attn_mid_b, "attn_b")
        peer_mid = [middle(x, "peer") for x in peer_pair]
        attn_a = jnp.where(at_end, attn_end_a, attn_mid_a)
        attn_b = jnp.where(at_end, attn_end_b, attn_mid_b)
        attn_xa = [turn(attn_a, "dp", s, "attn_xa") for s in steps]
        attn_xb = [turn(attn_b, "dp", s, "attn_xb") for s in steps]
        own_all = jnp.stack([own_1, own_2, jnp.where(at_end, own_end, own_mid)])
        own_all_s = swap(own_all, "own_s")
        peer_1s = [swap(x, "peer_1s") for x in peer_1]
        grad_q, grad_kv = backward(d_part)
        peer_send, (own_all_s, grad_kv, *rest) = gate(peer_mid, own_all_s, grad_kv, *peer_1s, *attn_x1)
        peer_1s, attn_x1 = rest[: n_dp - 1], rest[n_dp - 1 :]
        peer_end = [ends(x, "peer") for x in peer_send]
        peer_mid_s = [swap(x, "peer_mid_s") for x in peer_send]
        attn_all = jnp.stack([attn_1, jnp.where(at_end, attn_a, attn_b), jnp.where(at_end, attn_b, attn_a)])
        share = own_all.shape[0] * half
        rows = jnp.concatenate([own_rows, own_all.reshape(share, -1), own_all_s.reshape(share, -1)], 0)
        cols = [attn, attn_all[:, :half].reshape(share, -1), attn_all[:, half:].reshape(share, -1)]
        total = outer(rows, jnp.concatenate(cols, 0))
        for s in steps:
            rows = [peer[s - 1], peer_other[s - 1], peer_1[s - 1], peer_1s[s - 1]]
            total += outer(jnp.concatenate(rows, 0), jnp.concatenate([attn_x0[s - 1], attn_x1[s - 1]], 0))
        sent = send_home(grad_kv)
        peer_end, (total, *rest) = gate(peer_end, total, *attn_xa, *attn_xb)
        attn_xa, attn_xb = rest[: n_dp - 1], rest[n_dp - 1 :]
        for part, mid, end in ((0, peer_mid, peer_end), (1, peer_mid_s, [swap(x, "peer_end_s") for x in peer_end])):
            for s in steps:
                rows = lax.optimization_barrier(jnp.where(at_end, end[s - 1], mid[s - 1]))
                cols = [x[s - 1][part * half : (part + 1) * half] for x in (attn_xa, attn_xb)]
                total += outer(rows.reshape(2 * half, -1), jnp.concatenate(cols, 0))
        weight_grad = total.astype(jnp.bfloat16)
        sent, (weight_grad,) = gate(sent, weight_grad)
        out_kv = add_home(grad_kv, sent)
    out_k, out_v = out_kv[:, :kv_width], out_kv[:, kv_width:]
    return (grad_q[None], out_k[None], out_v[None], weight_grad)


def solution(mesh):
    placed = (
        P(("groups", "dp"), "ctx", "head"),
        P(("groups", "dp"), "ctx", "head"),
        P(("groups", "dp"), "ctx", "head"),
        P(("groups", "dp"), "ctx"),
        P(("groups", "dp"), "ctx"),
        P("dp", "head"),
        P(("groups", "dp"), "ctx", None),
    )
    return jax.shard_map(
        shards,
        mesh=mesh,
        in_specs=placed,
        out_specs=(
            P(("groups", "dp"), "ctx", "head"),
            P(("groups", "dp"), "ctx", "head"),
            P(("groups", "dp"), "ctx", "head"),
            P(("groups", "dp"), "head"),
        ),
        check_vma=False,
    )
```

```python
import functools

import jax
import jax.numpy as jnp
from jax import lax
from jax.experimental import pallas as pl
from jax.experimental.pallas import tpu as pltpu
from jax.sharding import PartitionSpec as P

HEAD_SIZE = 128
SUMMARY_TOKENS = 64
SCALE = HEAD_SIZE ** (-0.5)
NEG_FILL = -1e30
MARK = 20_000_000_000
VMEM_LIMIT = 48 * 1024 * 1024

VMEM = pltpu.MemorySpace.VMEM
SMEM = pltpu.MemorySpace.SMEM


def dot(a, b, contract):
    return lax.dot_general(a, b, (contract, ((), ())), preferred_element_type=jnp.float32)


def mask_bias(count_ref, id_column_ref, id_row_ref, shape, seg_len):
    rows = lax.broadcasted_iota(jnp.int32, shape, 0)
    cols = lax.broadcasted_iota(jnp.int32, shape, 1)
    own = (rows >= cols) & (id_column_ref[...] == id_row_ref[...])
    far = (cols >= seg_len) & (cols < seg_len + SUMMARY_TOKENS * count_ref[0, 0])
    return jnp.where(own | far, 0.0, NEG_FILL).astype(jnp.float32)


def softmax_rows(q_head, k_head, bias):
    scores = dot(q_head, k_head, ((1,), (1,))) * SCALE + bias
    top = jnp.max(scores, axis=-1, keepdims=True)
    expo = jnp.exp(scores - top)
    return expo / jnp.sum(expo, axis=-1, keepdims=True)


def forward_kernel(n_head, count_ref, idc_ref, idr_ref, q_ref, k_ref, v_ref, attn_ref, turned_ref, bias_ref):
    seg_len, q_width = q_ref.shape
    kv_heads = k_ref.shape[1] // HEAD_SIZE
    group = q_width // k_ref.shape[1]
    share = seg_len // n_head
    bias_ref[...] = mask_bias(count_ref, idc_ref, idr_ref, bias_ref.shape, seg_len)
    for kv in range(kv_heads):
        kv_cols = slice(kv * HEAD_SIZE, (kv + 1) * HEAD_SIZE)
        for g in range(group):
            h = kv * group + g
            cols = slice(h * HEAD_SIZE, (h + 1) * HEAD_SIZE)
            probs_b = softmax_rows(q_ref[:, cols], k_ref[:, kv_cols], bias_ref[...]).astype(jnp.bfloat16)
            attn = dot(probs_b, v_ref[:, kv_cols], ((1,), (0,))).astype(jnp.bfloat16)
            attn_ref[:, cols] = attn
            for core in range(n_head):
                to = lax.rem(core + n_head - count_ref[0, 1], n_head) * share
                turned_ref[pl.ds(pl.multiple_of(to, share), share), cols] = attn[core * share : (core + 1) * share]


def backward_kernel(count_ref, idc_ref, idr_ref, q_ref, k_ref, v_ref, attn_ref, d_mine_ref, d_part_ref, token_ref,
                    gq_ref, gkv_ref, bias_ref):
    seg_len, q_width = q_ref.shape
    kv_width = k_ref.shape[1]
    kv_heads = kv_width // HEAD_SIZE
    group = q_width // kv_width
    bias_ref[...] = mask_bias(count_ref, idc_ref, idr_ref, bias_ref.shape, seg_len)
    for kv in range(kv_heads):
        kv_cols = slice(kv * HEAD_SIZE, (kv + 1) * HEAD_SIZE)
        k_head = k_ref[:, kv_cols]
        v_head = v_ref[:, kv_cols]
        grad_k = jnp.zeros((k_ref.shape[0], HEAD_SIZE), jnp.float32)
        grad_v = jnp.zeros((k_ref.shape[0], HEAD_SIZE), jnp.float32)
        for g in range(group):
            h = kv * group + g
            cols = slice(h * HEAD_SIZE, (h + 1) * HEAD_SIZE)
            q_head = q_ref[:, cols]
            d_sum = d_mine_ref[:, cols]
            for part in range(d_part_ref.shape[0]):
                d_sum = d_sum + d_part_ref[part, :, cols].astype(jnp.float32)
            d_head = d_sum.astype(jnp.bfloat16)
            prob = softmax_rows(q_head, k_head, bias_ref[...])
            probs_b = prob.astype(jnp.bfloat16)
            delta = jnp.sum(
                d_head.astype(jnp.float32) * attn_ref[:, cols].astype(jnp.float32), axis=-1, keepdims=True
            )
            dprob = dot(d_head, v_head, ((1,), (1,)))
            ds_b = (prob * (dprob - delta)).astype(jnp.bfloat16)
            gq_ref[:, cols] = (SCALE * dot(ds_b, k_head, ((1,), (0,)))).astype(jnp.bfloat16)
            grad_k += dot(ds_b, q_head, ((0,), (0,)))
            grad_v += dot(probs_b, d_head, ((0,), (0,)))
        gkv_ref[:, kv_cols] = SCALE * grad_k
        gkv_ref[:, kv_width + kv * HEAD_SIZE : kv_width + (kv + 1) * HEAD_SIZE] = grad_v


def call_attention(kernel, out_shape, operands, bias_shape, flops):
    return pl.pallas_call(
        kernel,
        out_shape=out_shape,
        in_specs=[pl.BlockSpec(memory_space=SMEM)] + [pl.BlockSpec(memory_space=VMEM)] * (len(operands) - 1),
        out_specs=jax.tree.map(lambda _: pl.BlockSpec(memory_space=VMEM), out_shape),
        scratch_shapes=[pltpu.VMEM(bias_shape, jnp.float32)],
        compiler_params=pltpu.CompilerParams(vmem_limit_bytes=VMEM_LIMIT),
        cost_estimate=pl.CostEstimate(flops=flops, bytes_accessed=4 << 20, transcendentals=1 << 20),
    )(*operands)


def mark_kernel(*refs):
    refs[-1][...] = refs[0][...]


def mark(token, *done):
    return pl.pallas_call(
        mark_kernel,
        out_shape=jax.ShapeDtypeStruct(token.shape, token.dtype),
        in_specs=[pl.BlockSpec(memory_space=VMEM)] + [pl.BlockSpec(memory_space=pl.ANY)] * len(done),
        out_specs=pl.BlockSpec(memory_space=VMEM),
        cost_estimate=pl.CostEstimate(flops=MARK, bytes_accessed=0, transcendentals=0),
    )(token, *done)


def outer(rows, attn):
    contract = tuple(range(rows.ndim - 1))
    return dot(rows, attn, (contract, contract))


def turn(x, axis, step, name):
    n = lax.axis_size(axis)
    with jax.named_scope(name):
        return lax.ppermute(x, axis, [(i, (i + step) % n) for i in range(n)])


def line_pairs(n, step):
    return [(i, i + step) for i in range(n) if 0 <= i + step < n]


def pairs(x, name):
    with jax.named_scope(name + "_pairs"):
        return lax.ppermute(x, "ctx", [(0, 1), (1, 0), (2, 3), (3, 2)])


def middle(x, name):
    with jax.named_scope(name + "_middle"):
        return lax.ppermute(x, "ctx", [(1, 2), (2, 1)])


def two_away(x, name):
    with jax.named_scope(name + "_two"):
        return lax.ppermute(x, "ctx", [(0, 2), (1, 3), (2, 0), (3, 1)])


def ends(x, name):
    with jax.named_scope(name + "_ends"):
        return lax.ppermute(x, "ctx", [(1, 0), (2, 3)])


def gate(arrays, *done):
    out = lax.optimization_barrier((*arrays, *done))
    return list(out[: len(arrays)]), list(out[len(arrays) :])


def shards(queries, keys, values, tok_ids, vis_start, out_weight, grad_out):
    seg_len = queries.shape[1]
    kv_width = keys.shape[2]
    d_model = grad_out.shape[2]
    part_rows = out_weight.shape[0]
    n_ctx = lax.axis_size("ctx")
    n_dp = lax.axis_size("dp")
    n_head = lax.axis_size("head")
    place = lax.axis_index("ctx")
    me_dp = lax.axis_index("dp")
    me_head = lax.axis_index("head")
    half = seg_len // n_head
    cut = seg_len - SUMMARY_TOKENS

    tail = jnp.concatenate([keys[0, cut:], values[0, cut:]], axis=1)
    far = [lax.ppermute(tail, "ctx", line_pairs(n_ctx, s)) for s in range(1, n_ctx)]
    far_len = -(-(n_ctx - 1) * SUMMARY_TOKENS // HEAD_SIZE) * HEAD_SIZE
    far.append(jnp.zeros((far_len - (n_ctx - 1) * SUMMARY_TOKENS, 2 * kv_width), keys.dtype))
    far = jnp.concatenate(far, axis=0)
    n_keys = seg_len + far_len

    wide = n_ctx != 4
    token = jnp.zeros((8, 128), jnp.float32)

    def rows_of(core, dp):
        return lax.dynamic_slice(grad_out[0], (core * half, dp * part_rows), (half, part_rows))

    own = rows_of(me_head, me_dp)
    (own_late,), (far,) = gate([own], far)
    peer, peer_other = [], []
    for s in range(1, n_dp):
        to = lax.rem(me_dp + s, n_dp)
        peer.append(turn(rows_of(me_head, to), "dp", s, "peer_in"))

    all_keys = jnp.concatenate([keys[0], far[:, :kv_width]], axis=0)
    all_vals = jnp.concatenate([values[0], far[:, kv_width:]], axis=0)
    count = jnp.stack([place - vis_start[0, 0], me_head]).reshape(1, 2).astype(jnp.int32)
    id_column = tok_ids[0].reshape(seg_len, 1)
    id_row = jnp.pad(tok_ids, ((0, 0), (0, far_len)), constant_values=-1)
    pair_flops = 2 * seg_len * n_keys * queries.shape[2]
    attn, turned = call_attention(
        functools.partial(forward_kernel, n_head),
        (jax.ShapeDtypeStruct(queries.shape[1:], jnp.bfloat16),) * 2,
        (count, id_column, id_row, queries[0], all_keys, all_vals),
        (seg_len, n_keys),
        2 * pair_flops,
    )

    peer, (attn,) = gate(peer, attn)
    peer_other = [turn(x, "head", 1, "peer_s") for x in peer]
    first_core = me_head == 0
    parts = []
    for s in range(1, n_dp):
        mine, other = peer[s - 1], peer_other[s - 1]
        rows = jnp.concatenate([jnp.where(first_core, mine, other), jnp.where(first_core, other, mine)], 0)
        parts.append(jnp.dot(rows, out_weight, preferred_element_type=jnp.float32).astype(jnp.bfloat16))
    back = [turn(part, "dp", -s, "back") for s, part in zip(range(1, n_dp), parts)]
    own_rows = lax.dynamic_slice(grad_out[0], (0, me_dp * part_rows), (seg_len, part_rows))
    (own_rows,), back = gate([own_rows], *back)
    d_mine = jnp.dot(own_rows, out_weight, preferred_element_type=jnp.float32)
    d_part = jnp.stack(back)

    def backward(d_part):
        return call_attention(
            backward_kernel,
            (
                jax.ShapeDtypeStruct(queries.shape[1:], jnp.bfloat16),
                jax.ShapeDtypeStruct((n_keys, 2 * kv_width), jnp.float32),
            ),
            (count, id_column, id_row, queries[0], all_keys, all_vals, attn, d_mine, d_part, token),
            (seg_len, n_keys),
            5 * pair_flops,
        )


    def send_home(grad_kv):
        sent = []
        for s in range(1, n_ctx):
            begin = seg_len + (s - 1) * SUMMARY_TOKENS
            with jax.named_scope("grads"):
                sent.append(lax.ppermute(grad_kv[begin : begin + SUMMARY_TOKENS], "ctx", line_pairs(n_ctx, -s)))
        return sent

    def add_home(grad_kv, sent):
        home = sum(sent, grad_kv[cut:seg_len])
        return jnp.concatenate([grad_kv[:cut], home], 0).astype(jnp.bfloat16)

    if wide:
        grad_q, grad_kv = backward(d_part)
        out_kv = add_home(grad_kv, send_home(grad_kv))
        block = d_model // (n_ctx * n_dp)
        columns = (
            grad_out[0].reshape(seg_len, n_dp, n_ctx, block).transpose(0, 2, 1, 3).reshape(seg_len, d_model)
        )
        shard = lax.psum_scatter(
            jnp.einsum("sd,se->de", columns, attn, preferred_element_type=jnp.float32),
            ("ctx", "dp"),
            scatter_dimension=0,
            tiled=True,
        ).astype(jnp.bfloat16)
        weight_grad = lax.all_gather(shard, "ctx", axis=0, tiled=True)
    else:
        steps = range(1, n_dp)
        at_end = (place == 0) | (place == n_ctx - 1)

        def swap(x, name):
            return turn(x, "head", 1, name)

        own_1 = pairs(own, "own")
        own_2 = two_away(own_late, "own")
        own_mid = middle(own_late, "own")
        attn_1 = pairs(turned, "attn")
        attn_x0 = [turn(turned, "dp", s, "attn_x0") for s in steps]
        token = mark(token, own_1, own_2, own_mid)
        (attn_0, own_2, *peer), (token,) = gate([turned, own_2, *peer], token)
        own_end = ends(own_2, "own")
        peer_1 = [pairs(x, "peer") for x in peer]
        attn_mid_a = middle(attn_0, "attn_a")
        token = mark(token)
        (attn_1,), (token,) = gate([attn_1], token)
        attn_mid_b = middle(attn_1, "attn_b")
        attn_end_a = ends(attn_mid_a, "attn_a")
        attn_x1 = [turn(attn_1, "dp", s, "attn_x1") for s in steps]
        peer_pair = [jnp.stack([a, b]) for a, b in zip(peer, peer_1)]
        peer_pair, (attn_mid_b, own_end, *rest) = gate(peer_pair, attn_mid_b, own_end, *parts, *attn_x0)
        attn_x0 = rest[n_dp - 1 :]
        attn_end_b = ends(attn_mid_b, "attn_b")
        peer_mid = [middle(x, "peer") for x in peer_pair]
        attn_a = jnp.where(at_end, attn_end_a, attn_mid_a)
        attn_b = jnp.where(at_end, attn_end_b, attn_mid_b)
        attn_xa = [turn(attn_a, "dp", s, "attn_xa") for s in steps]
        attn_xb = [turn(attn_b, "dp", s, "attn_xb") for s in steps]
        peer_1s = [swap(x, "peer_1s") for x in peer_1]
        grad_q, grad_kv = backward(d_part)
        (own_1, own_end), (grad_kv,) = gate([own_1, own_end], grad_kv)
        own_all = jnp.stack([own_1, own_2, jnp.where(at_end, own_end, own_mid)])
        own_all_s = swap(own_all, "own_s")
        peer_send, (grad_kv, *rest) = gate(peer_mid, grad_kv, *peer_1s, *attn_x1)
        peer_1s, attn_x1 = rest[: n_dp - 1], rest[n_dp - 1 :]
        peer_end = [ends(x, "peer") for x in peer_send]
        peer_mid_s = [swap(x, "peer_mid_s") for x in peer_send]
        attn_all = jnp.stack([attn_1, jnp.where(at_end, attn_a, attn_b), jnp.where(at_end, attn_b, attn_a)])
        share = own_all.shape[0] * half
        rows = jnp.concatenate([own_rows, own_all.reshape(share, -1), own_all_s.reshape(share, -1)], 0)
        cols = [attn, attn_all[:, :half].reshape(share, -1), attn_all[:, half:].reshape(share, -1)]
        total = outer(rows, jnp.concatenate(cols, 0))
        for s in steps:
            rows = [peer[s - 1], peer_other[s - 1], peer_1[s - 1], peer_1s[s - 1]]
            total += outer(jnp.concatenate(rows, 0), jnp.concatenate([attn_x0[s - 1], attn_x1[s - 1]], 0))
        sent = send_home(grad_kv)
        peer_end, (total, *rest) = gate(peer_end, total, *attn_xa, *attn_xb)
        attn_xa, attn_xb = rest[: n_dp - 1], rest[n_dp - 1 :]
        for part, mid, end in ((0, peer_mid, peer_end), (1, peer_mid_s, [swap(x, "peer_end_s") for x in peer_end])):
            for s in steps:
                rows = lax.optimization_barrier(jnp.where(at_end, end[s - 1], mid[s - 1]))
                cols = [x[s - 1][part * half : (part + 1) * half] for x in (attn_xa, attn_xb)]
                total += outer(rows.reshape(2 * half, -1), jnp.concatenate(cols, 0))
        weight_grad = total.astype(jnp.bfloat16)
        sent, (weight_grad,) = gate(sent, weight_grad)
        out_kv = add_home(grad_kv, sent)
    out_k, out_v = out_kv[:, :kv_width], out_kv[:, kv_width:]
    return (grad_q[None], out_k[None], out_v[None], weight_grad)


def solution(mesh):
    placed = (
        P(("groups", "dp"), "ctx", "head"),
        P(("groups", "dp"), "ctx", "head"),
        P(("groups", "dp"), "ctx", "head"),
        P(("groups", "dp"), "ctx"),
        P(("groups", "dp"), "ctx"),
        P("dp", "head"),
        P(("groups", "dp"), "ctx", None),
    )
    return jax.shard_map(
        shards,
        mesh=mesh,
        in_specs=placed,
        out_specs=(
            P(("groups", "dp"), "ctx", "head"),
            P(("groups", "dp"), "ctx", "head"),
            P(("groups", "dp"), "ctx", "head"),
            P(("groups", "dp"), "head"),
        ),
        check_vma=False,
    )
```

```python
import functools

import jax
import jax.numpy as jnp
from jax import lax
from jax.experimental import pallas as pl
from jax.experimental.pallas import tpu as pltpu
from jax.sharding import PartitionSpec as P

HEAD_SIZE = 128
SUMMARY_TOKENS = 64
SCALE = HEAD_SIZE ** (-0.5)
NEG_FILL = -1e30
MARK = 20_000_000_000
VMEM_LIMIT = 48 * 1024 * 1024

VMEM = pltpu.MemorySpace.VMEM
SMEM = pltpu.MemorySpace.SMEM


def dot(a, b, contract):
    return lax.dot_general(a, b, (contract, ((), ())), preferred_element_type=jnp.float32)


def mask_bias(count_ref, id_column_ref, id_row_ref, shape, seg_len):
    rows = lax.broadcasted_iota(jnp.int32, shape, 0)
    cols = lax.broadcasted_iota(jnp.int32, shape, 1)
    own = (rows >= cols) & (id_column_ref[...] == id_row_ref[...])
    far = (cols >= seg_len) & (cols < seg_len + SUMMARY_TOKENS * count_ref[0, 0])
    return jnp.where(own | far, 0.0, NEG_FILL).astype(jnp.float32)


def softmax_rows(q_head, k_head, bias):
    scores = dot(q_head, k_head, ((1,), (1,))) * SCALE + bias
    top = jnp.max(scores, axis=-1, keepdims=True)
    expo = jnp.exp(scores - top)
    return expo / jnp.sum(expo, axis=-1, keepdims=True)


def forward_kernel(n_head, count_ref, idc_ref, idr_ref, q_ref, k_ref, v_ref, attn_ref, turned_ref, bias_ref):
    seg_len, q_width = q_ref.shape
    kv_heads = k_ref.shape[1] // HEAD_SIZE
    group = q_width // k_ref.shape[1]
    share = seg_len // n_head
    bias_ref[...] = mask_bias(count_ref, idc_ref, idr_ref, bias_ref.shape, seg_len)
    for kv in range(kv_heads):
        kv_cols = slice(kv * HEAD_SIZE, (kv + 1) * HEAD_SIZE)
        for g in range(group):
            h = kv * group + g
            cols = slice(h * HEAD_SIZE, (h + 1) * HEAD_SIZE)
            probs_b = softmax_rows(q_ref[:, cols], k_ref[:, kv_cols], bias_ref[...]).astype(jnp.bfloat16)
            attn = dot(probs_b, v_ref[:, kv_cols], ((1,), (0,))).astype(jnp.bfloat16)
            attn_ref[:, cols] = attn
            for core in range(n_head):
                to = lax.rem(core + n_head - count_ref[0, 1], n_head) * share
                turned_ref[pl.ds(pl.multiple_of(to, share), share), cols] = attn[core * share : (core + 1) * share]


def backward_kernel(count_ref, idc_ref, idr_ref, q_ref, k_ref, v_ref, attn_ref, d_mine_ref, d_part_ref, token_ref,
                    gq_ref, gkv_ref, bias_ref):
    seg_len, q_width = q_ref.shape
    kv_width = k_ref.shape[1]
    kv_heads = kv_width // HEAD_SIZE
    group = q_width // kv_width
    bias_ref[...] = mask_bias(count_ref, idc_ref, idr_ref, bias_ref.shape, seg_len)
    for kv in range(kv_heads):
        kv_cols = slice(kv * HEAD_SIZE, (kv + 1) * HEAD_SIZE)
        k_head = k_ref[:, kv_cols]
        v_head = v_ref[:, kv_cols]
        grad_k = jnp.zeros((k_ref.shape[0], HEAD_SIZE), jnp.float32)
        grad_v = jnp.zeros((k_ref.shape[0], HEAD_SIZE), jnp.float32)
        for g in range(group):
            h = kv * group + g
            cols = slice(h * HEAD_SIZE, (h + 1) * HEAD_SIZE)
            q_head = q_ref[:, cols]
            d_sum = d_mine_ref[:, cols]
            for part in range(d_part_ref.shape[0]):
                d_sum = d_sum + d_part_ref[part, :, cols].astype(jnp.float32)
            d_head = d_sum.astype(jnp.bfloat16)
            prob = softmax_rows(q_head, k_head, bias_ref[...])
            probs_b = prob.astype(jnp.bfloat16)
            delta = jnp.sum(
                d_head.astype(jnp.float32) * attn_ref[:, cols].astype(jnp.float32), axis=-1, keepdims=True
            )
            dprob = dot(d_head, v_head, ((1,), (1,)))
            ds_b = (prob * (dprob - delta)).astype(jnp.bfloat16)
            gq_ref[:, cols] = (SCALE * dot(ds_b, k_head, ((1,), (0,)))).astype(jnp.bfloat16)
            grad_k += dot(ds_b, q_head, ((0,), (0,)))
            grad_v += dot(probs_b, d_head, ((0,), (0,)))
        gkv_ref[:, kv_cols] = SCALE * grad_k
        gkv_ref[:, kv_width + kv * HEAD_SIZE : kv_width + (kv + 1) * HEAD_SIZE] = grad_v


def call_attention(kernel, out_shape, operands, bias_shape, flops):
    return pl.pallas_call(
        kernel,
        out_shape=out_shape,
        in_specs=[pl.BlockSpec(memory_space=SMEM)] + [pl.BlockSpec(memory_space=VMEM)] * (len(operands) - 1),
        out_specs=jax.tree.map(lambda _: pl.BlockSpec(memory_space=VMEM), out_shape),
        scratch_shapes=[pltpu.VMEM(bias_shape, jnp.float32)],
        compiler_params=pltpu.CompilerParams(vmem_limit_bytes=VMEM_LIMIT),
        cost_estimate=pl.CostEstimate(flops=flops, bytes_accessed=4 << 20, transcendentals=1 << 20),
    )(*operands)


def mark_kernel(*refs):
    refs[-1][...] = refs[0][...]


def mark(token, *done):
    return pl.pallas_call(
        mark_kernel,
        out_shape=jax.ShapeDtypeStruct(token.shape, token.dtype),
        in_specs=[pl.BlockSpec(memory_space=VMEM)] + [pl.BlockSpec(memory_space=pl.ANY)] * len(done),
        out_specs=pl.BlockSpec(memory_space=VMEM),
        cost_estimate=pl.CostEstimate(flops=MARK, bytes_accessed=0, transcendentals=0),
    )(token, *done)


def outer(rows, attn):
    contract = tuple(range(rows.ndim - 1))
    return dot(rows, attn, (contract, contract))


def turn(x, axis, step, name):
    n = lax.axis_size(axis)
    with jax.named_scope(name):
        return lax.ppermute(x, axis, [(i, (i + step) % n) for i in range(n)])


def line_pairs(n, step):
    return [(i, i + step) for i in range(n) if 0 <= i + step < n]


def pairs(x, name):
    with jax.named_scope(name + "_pairs"):
        return lax.ppermute(x, "ctx", [(0, 1), (1, 0), (2, 3), (3, 2)])


def middle(x, name):
    with jax.named_scope(name + "_middle"):
        return lax.ppermute(x, "ctx", [(1, 2), (2, 1)])


def two_away(x, name):
    with jax.named_scope(name + "_two"):
        return lax.ppermute(x, "ctx", [(0, 2), (1, 3), (2, 0), (3, 1)])


def ends(x, name):
    with jax.named_scope(name + "_ends"):
        return lax.ppermute(x, "ctx", [(1, 0), (2, 3)])


def gate(arrays, *done):
    out = lax.optimization_barrier((*arrays, *done))
    return list(out[: len(arrays)]), list(out[len(arrays) :])


def shards(queries, keys, values, tok_ids, vis_start, out_weight, grad_out):
    seg_len = queries.shape[1]
    kv_width = keys.shape[2]
    d_model = grad_out.shape[2]
    part_rows = out_weight.shape[0]
    n_ctx = lax.axis_size("ctx")
    n_dp = lax.axis_size("dp")
    n_head = lax.axis_size("head")
    place = lax.axis_index("ctx")
    me_dp = lax.axis_index("dp")
    me_head = lax.axis_index("head")
    half = seg_len // n_head
    cut = seg_len - SUMMARY_TOKENS

    tail = jnp.concatenate([keys[0, cut:], values[0, cut:]], axis=1)
    far = [lax.ppermute(tail, "ctx", line_pairs(n_ctx, s)) for s in range(1, n_ctx)]
    far_len = -(-(n_ctx - 1) * SUMMARY_TOKENS // HEAD_SIZE) * HEAD_SIZE
    far.append(jnp.zeros((far_len - (n_ctx - 1) * SUMMARY_TOKENS, 2 * kv_width), keys.dtype))
    far = jnp.concatenate(far, axis=0)
    n_keys = seg_len + far_len

    wide = n_ctx != 4
    token = jnp.zeros((8, 128), jnp.float32)

    def rows_of(core, dp):
        return lax.dynamic_slice(grad_out[0], (core * half, dp * part_rows), (half, part_rows))

    own = rows_of(me_head, me_dp)
    (own_late,), (far,) = gate([own], far)
    peer, peer_other = [], []
    for s in range(1, n_dp):
        to = lax.rem(me_dp + s, n_dp)
        peer.append(turn(rows_of(me_head, to), "dp", s, "peer_in"))

    all_keys = jnp.concatenate([keys[0], far[:, :kv_width]], axis=0)
    all_vals = jnp.concatenate([values[0], far[:, kv_width:]], axis=0)
    count = jnp.stack([place - vis_start[0, 0], me_head]).reshape(1, 2).astype(jnp.int32)
    id_column = tok_ids[0].reshape(seg_len, 1)
    id_row = jnp.pad(tok_ids, ((0, 0), (0, far_len)), constant_values=-1)
    pair_flops = 2 * seg_len * n_keys * queries.shape[2]
    attn, turned = call_attention(
        functools.partial(forward_kernel, n_head),
        (jax.ShapeDtypeStruct(queries.shape[1:], jnp.bfloat16),) * 2,
        (count, id_column, id_row, queries[0], all_keys, all_vals),
        (seg_len, n_keys),
        2 * pair_flops,
    )

    peer, (attn,) = gate(peer, attn)
    peer_other = [turn(x, "head", 1, "peer_s") for x in peer]
    first_core = me_head == 0
    parts = []
    for s in range(1, n_dp):
        mine, other = peer[s - 1], peer_other[s - 1]
        rows = jnp.concatenate([jnp.where(first_core, mine, other), jnp.where(first_core, other, mine)], 0)
        parts.append(jnp.dot(rows, out_weight, preferred_element_type=jnp.float32).astype(jnp.bfloat16))
    back = [turn(part, "dp", -s, "back") for s, part in zip(range(1, n_dp), parts)]
    own_rows = lax.dynamic_slice(grad_out[0], (0, me_dp * part_rows), (seg_len, part_rows))
    (own_rows,), back = gate([own_rows], *back)
    d_mine = jnp.dot(own_rows, out_weight, preferred_element_type=jnp.float32)
    d_part = jnp.stack(back)

    def backward(d_part):
        return call_attention(
            backward_kernel,
            (
                jax.ShapeDtypeStruct(queries.shape[1:], jnp.bfloat16),
                jax.ShapeDtypeStruct((n_keys, 2 * kv_width), jnp.float32),
            ),
            (count, id_column, id_row, queries[0], all_keys, all_vals, attn, d_mine, d_part, token),
            (seg_len, n_keys),
            5 * pair_flops,
        )


    def send_home(grad_kv):
        sent = []
        for s in range(1, n_ctx):
            begin = seg_len + (s - 1) * SUMMARY_TOKENS
            part = grad_kv[begin : begin + SUMMARY_TOKENS].astype(jnp.bfloat16)
            with jax.named_scope("grads"):
                sent.append(lax.ppermute(part, "ctx", line_pairs(n_ctx, -s)))
        return sent

    def add_home(grad_kv, sent):
        home = sum([x.astype(jnp.float32) for x in sent], grad_kv[cut:seg_len])
        return jnp.concatenate([grad_kv[:cut], home], 0).astype(jnp.bfloat16)

    if wide:
        grad_q, grad_kv = backward(d_part)
        out_kv = add_home(grad_kv, send_home(grad_kv))
        block = d_model // (n_ctx * n_dp)
        columns = (
            grad_out[0].reshape(seg_len, n_dp, n_ctx, block).transpose(0, 2, 1, 3).reshape(seg_len, d_model)
        )
        shard = lax.psum_scatter(
            jnp.einsum("sd,se->de", columns, attn, preferred_element_type=jnp.float32),
            ("ctx", "dp"),
            scatter_dimension=0,
            tiled=True,
        ).astype(jnp.bfloat16)
        weight_grad = lax.all_gather(shard, "ctx", axis=0, tiled=True)
    else:
        steps = range(1, n_dp)
        at_end = (place == 0) | (place == n_ctx - 1)

        def swap(x, name):
            return turn(x, "head", 1, name)

        own_1 = pairs(own, "own")
        own_2 = two_away(own_late, "own")
        own_mid = middle(own_late, "own")
        attn_1 = pairs(turned, "attn")
        attn_x0 = [turn(turned, "dp", s, "attn_x0") for s in steps]
        token = mark(token, own_1, own_2, own_mid)
        (attn_0, own_2, *peer), (token,) = gate([turned, own_2, *peer], token)
        own_end = ends(own_2, "own")
        peer_1 = [pairs(x, "peer") for x in peer]
        attn_mid_a = middle(attn_0, "attn_a")
        token = mark(token)
        (attn_1,), (token,) = gate([attn_1], token)
        attn_mid_b = middle(attn_1, "attn_b")
        attn_end_a = ends(attn_mid_a, "attn_a")
        attn_x1 = [turn(attn_1, "dp", s, "attn_x1") for s in steps]
        peer_pair = [jnp.stack([a, b]) for a, b in zip(peer, peer_1)]
        peer_pair, (attn_mid_b, own_end, *rest) = gate(peer_pair, attn_mid_b, own_end, *parts, *attn_x0)
        attn_x0 = rest[n_dp - 1 :]
        attn_end_b = ends(attn_mid_b, "attn_b")
        peer_mid = [middle(x, "peer") for x in peer_pair]
        attn_a = jnp.where(at_end, attn_end_a, attn_mid_a)
        attn_b = jnp.where(at_end, attn_end_b, attn_mid_b)
        attn_xa = [turn(attn_a, "dp", s, "attn_xa") for s in steps]
        attn_xb = [turn(attn_b, "dp", s, "attn_xb") for s in steps]
        peer_1s = [swap(x, "peer_1s") for x in peer_1]
        grad_q, grad_kv = backward(d_part)
        (own_1, own_end), (grad_kv,) = gate([own_1, own_end], grad_kv)
        own_all = jnp.stack([own_1, own_2, jnp.where(at_end, own_end, own_mid)])
        own_all_s = swap(own_all, "own_s")
        peer_send, (grad_kv, *rest) = gate(peer_mid, grad_kv, *peer_1s, *attn_x1)
        peer_1s, attn_x1 = rest[: n_dp - 1], rest[n_dp - 1 :]
        peer_end = [ends(x, "peer") for x in peer_send]
        peer_mid_s = [swap(x, "peer_mid_s") for x in peer_send]
        attn_all = jnp.stack([attn_1, jnp.where(at_end, attn_a, attn_b), jnp.where(at_end, attn_b, attn_a)])
        share = own_all.shape[0] * half
        rows = jnp.concatenate([own_rows, own_all.reshape(share, -1), own_all_s.reshape(share, -1)], 0)
        cols = [attn, attn_all[:, :half].reshape(share, -1), attn_all[:, half:].reshape(share, -1)]
        total = outer(rows, jnp.concatenate(cols, 0))
        for s in steps:
            rows = [peer[s - 1], peer_other[s - 1], peer_1[s - 1], peer_1s[s - 1]]
            total += outer(jnp.concatenate(rows, 0), jnp.concatenate([attn_x0[s - 1], attn_x1[s - 1]], 0))
        sent = send_home(grad_kv)
        peer_end, (total, *rest) = gate(peer_end, total, *attn_xa, *attn_xb)
        attn_xa, attn_xb = rest[: n_dp - 1], rest[n_dp - 1 :]
        for part, mid, end in ((0, peer_mid, peer_end), (1, peer_mid_s, [swap(x, "peer_end_s") for x in peer_end])):
            for s in steps:
                rows = lax.optimization_barrier(jnp.where(at_end, end[s - 1], mid[s - 1]))
                cols = [x[s - 1][part * half : (part + 1) * half] for x in (attn_xa, attn_xb)]
                total += outer(rows.reshape(2 * half, -1), jnp.concatenate(cols, 0))
        weight_grad = total.astype(jnp.bfloat16)
        sent, (weight_grad,) = gate(sent, weight_grad)
        out_kv = add_home(grad_kv, sent)
    out_k, out_v = out_kv[:, :kv_width], out_kv[:, kv_width:]
    return (grad_q[None], out_k[None], out_v[None], weight_grad)


def solution(mesh):
    placed = (
        P(("groups", "dp"), "ctx", "head"),
        P(("groups", "dp"), "ctx", "head"),
        P(("groups", "dp"), "ctx", "head"),
        P(("groups", "dp"), "ctx"),
        P(("groups", "dp"), "ctx"),
        P("dp", "head"),
        P(("groups", "dp"), "ctx", None),
    )
    return jax.shard_map(
        shards,
        mesh=mesh,
        in_specs=placed,
        out_specs=(
            P(("groups", "dp"), "ctx", "head"),
            P(("groups", "dp"), "ctx", "head"),
            P(("groups", "dp"), "ctx", "head"),
            P(("groups", "dp"), "head"),
        ),
        check_vma=False,
    )
```

```python
import functools

import jax
import jax.numpy as jnp
from jax import lax
from jax.experimental import pallas as pl
from jax.experimental.pallas import tpu as pltpu
from jax.sharding import PartitionSpec as P

HEAD_SIZE = 128
SUMMARY_TOKENS = 64
SCALE = HEAD_SIZE ** (-0.5)
NEG_FILL = -1e30
MARK = 20_000_000_000
VMEM_LIMIT = 48 * 1024 * 1024

VMEM = pltpu.MemorySpace.VMEM
SMEM = pltpu.MemorySpace.SMEM


def dot(a, b, contract):
    return lax.dot_general(a, b, (contract, ((), ())), preferred_element_type=jnp.float32)


def mask_bias(count_ref, id_column_ref, id_row_ref, shape, seg_len):
    rows = lax.broadcasted_iota(jnp.int32, shape, 0)
    cols = lax.broadcasted_iota(jnp.int32, shape, 1)
    own = (rows >= cols) & (id_column_ref[...] == id_row_ref[...])
    far = (cols >= seg_len) & (cols < seg_len + SUMMARY_TOKENS * count_ref[0, 0])
    return jnp.where(own | far, 0.0, NEG_FILL).astype(jnp.float32)


def softmax_rows(q_head, k_head, bias):
    scores = dot(q_head, k_head, ((1,), (1,))) * SCALE + bias
    top = jnp.max(scores, axis=-1, keepdims=True)
    expo = jnp.exp(scores - top)
    return expo / jnp.sum(expo, axis=-1, keepdims=True)


def forward_kernel(n_head, count_ref, idc_ref, idr_ref, q_ref, k_ref, v_ref, attn_ref, turned_ref, bias_ref):
    seg_len, q_width = q_ref.shape
    kv_heads = k_ref.shape[1] // HEAD_SIZE
    group = q_width // k_ref.shape[1]
    share = seg_len // n_head
    bias_ref[...] = mask_bias(count_ref, idc_ref, idr_ref, bias_ref.shape, seg_len)
    for kv in range(kv_heads):
        kv_cols = slice(kv * HEAD_SIZE, (kv + 1) * HEAD_SIZE)
        for g in range(group):
            h = kv * group + g
            cols = slice(h * HEAD_SIZE, (h + 1) * HEAD_SIZE)
            probs_b = softmax_rows(q_ref[:, cols], k_ref[:, kv_cols], bias_ref[...]).astype(jnp.bfloat16)
            attn = dot(probs_b, v_ref[:, kv_cols], ((1,), (0,))).astype(jnp.bfloat16)
            attn_ref[:, cols] = attn
            for core in range(n_head):
                to = lax.rem(core + n_head - count_ref[0, 1], n_head) * share
                turned_ref[pl.ds(pl.multiple_of(to, share), share), cols] = attn[core * share : (core + 1) * share]


def backward_kernel(count_ref, idc_ref, idr_ref, q_ref, k_ref, v_ref, attn_ref, d_mine_ref, d_part_ref, token_ref,
                    gq_ref, gkv_ref, bias_ref):
    seg_len, q_width = q_ref.shape
    kv_width = k_ref.shape[1]
    kv_heads = kv_width // HEAD_SIZE
    group = q_width // kv_width
    bias_ref[...] = mask_bias(count_ref, idc_ref, idr_ref, bias_ref.shape, seg_len)
    for kv in range(kv_heads):
        kv_cols = slice(kv * HEAD_SIZE, (kv + 1) * HEAD_SIZE)
        k_head = k_ref[:, kv_cols]
        v_head = v_ref[:, kv_cols]
        grad_k = jnp.zeros((k_ref.shape[0], HEAD_SIZE), jnp.float32)
        grad_v = jnp.zeros((k_ref.shape[0], HEAD_SIZE), jnp.float32)
        for g in range(group):
            h = kv * group + g
            cols = slice(h * HEAD_SIZE, (h + 1) * HEAD_SIZE)
            q_head = q_ref[:, cols]
            d_sum = d_mine_ref[:, cols]
            for part in range(d_part_ref.shape[0]):
                d_sum = d_sum + d_part_ref[part, :, cols].astype(jnp.float32)
            d_head = d_sum.astype(jnp.bfloat16)
            prob = softmax_rows(q_head, k_head, bias_ref[...])
            probs_b = prob.astype(jnp.bfloat16)
            delta = jnp.sum(
                d_head.astype(jnp.float32) * attn_ref[:, cols].astype(jnp.float32), axis=-1, keepdims=True
            )
            dprob = dot(d_head, v_head, ((1,), (1,)))
            ds_b = (prob * (dprob - delta)).astype(jnp.bfloat16)
            gq_ref[:, cols] = (SCALE * dot(ds_b, k_head, ((1,), (0,)))).astype(jnp.bfloat16)
            grad_k += dot(ds_b, q_head, ((0,), (0,)))
            grad_v += dot(probs_b, d_head, ((0,), (0,)))
        gkv_ref[:, kv_cols] = SCALE * grad_k
        gkv_ref[:, kv_width + kv * HEAD_SIZE : kv_width + (kv + 1) * HEAD_SIZE] = grad_v


def call_attention(kernel, out_shape, operands, bias_shape, flops):
    return pl.pallas_call(
        kernel,
        out_shape=out_shape,
        in_specs=[pl.BlockSpec(memory_space=SMEM)] + [pl.BlockSpec(memory_space=VMEM)] * (len(operands) - 1),
        out_specs=jax.tree.map(lambda _: pl.BlockSpec(memory_space=VMEM), out_shape),
        scratch_shapes=[pltpu.VMEM(bias_shape, jnp.float32)],
        compiler_params=pltpu.CompilerParams(vmem_limit_bytes=VMEM_LIMIT),
        cost_estimate=pl.CostEstimate(flops=flops, bytes_accessed=4 << 20, transcendentals=1 << 20),
    )(*operands)


def mark_kernel(*refs):
    refs[-1][...] = refs[0][...]


def mark(token, *done):
    return pl.pallas_call(
        mark_kernel,
        out_shape=jax.ShapeDtypeStruct(token.shape, token.dtype),
        in_specs=[pl.BlockSpec(memory_space=VMEM)] + [pl.BlockSpec(memory_space=pl.ANY)] * len(done),
        out_specs=pl.BlockSpec(memory_space=VMEM),
        cost_estimate=pl.CostEstimate(flops=MARK, bytes_accessed=0, transcendentals=0),
    )(token, *done)


def outer(rows, attn):
    contract = tuple(range(rows.ndim - 1))
    return dot(rows, attn, (contract, contract))


def turn(x, axis, step, name):
    n = lax.axis_size(axis)
    with jax.named_scope(name):
        return lax.ppermute(x, axis, [(i, (i + step) % n) for i in range(n)])


def line_pairs(n, step):
    return [(i, i + step) for i in range(n) if 0 <= i + step < n]


def pairs(x, name):
    with jax.named_scope(name + "_pairs"):
        return lax.ppermute(x, "ctx", [(0, 1), (1, 0), (2, 3), (3, 2)])


def middle(x, name):
    with jax.named_scope(name + "_middle"):
        return lax.ppermute(x, "ctx", [(1, 2), (2, 1)])


def two_away(x, name):
    with jax.named_scope(name + "_two"):
        return lax.ppermute(x, "ctx", [(0, 2), (1, 3), (2, 0), (3, 1)])


def ends(x, name):
    with jax.named_scope(name + "_ends"):
        return lax.ppermute(x, "ctx", [(1, 0), (2, 3)])


def gate(arrays, *done):
    out = lax.optimization_barrier((*arrays, *done))
    return list(out[: len(arrays)]), list(out[len(arrays) :])


def shards(queries, keys, values, tok_ids, vis_start, out_weight, grad_out):
    seg_len = queries.shape[1]
    kv_width = keys.shape[2]
    d_model = grad_out.shape[2]
    part_rows = out_weight.shape[0]
    n_ctx = lax.axis_size("ctx")
    n_dp = lax.axis_size("dp")
    n_head = lax.axis_size("head")
    place = lax.axis_index("ctx")
    me_dp = lax.axis_index("dp")
    me_head = lax.axis_index("head")
    half = seg_len // n_head
    cut = seg_len - SUMMARY_TOKENS

    tail = jnp.concatenate([keys[0, cut:], values[0, cut:]], axis=1)
    far = [lax.ppermute(tail, "ctx", line_pairs(n_ctx, s)) for s in range(1, n_ctx)]
    far_len = -(-(n_ctx - 1) * SUMMARY_TOKENS // HEAD_SIZE) * HEAD_SIZE
    far.append(jnp.zeros((far_len - (n_ctx - 1) * SUMMARY_TOKENS, 2 * kv_width), keys.dtype))
    far = jnp.concatenate(far, axis=0)
    n_keys = seg_len + far_len

    wide = n_ctx != 4
    token = jnp.zeros((8, 128), jnp.float32)

    def rows_of(core, dp):
        return lax.dynamic_slice(grad_out[0], (core * half, dp * part_rows), (half, part_rows))

    own = rows_of(me_head, me_dp)
    (own_late,), (far,) = gate([own], far)
    peer, peer_other = [], []
    for s in range(1, n_dp):
        to = lax.rem(me_dp + s, n_dp)
        peer.append(turn(rows_of(me_head, to), "dp", s, "peer_in"))

    all_keys = jnp.concatenate([keys[0], far[:, :kv_width]], axis=0)
    all_vals = jnp.concatenate([values[0], far[:, kv_width:]], axis=0)
    count = jnp.stack([place - vis_start[0, 0], me_head]).reshape(1, 2).astype(jnp.int32)
    id_column = tok_ids[0].reshape(seg_len, 1)
    id_row = jnp.pad(tok_ids, ((0, 0), (0, far_len)), constant_values=-1)
    pair_flops = 2 * seg_len * n_keys * queries.shape[2]
    attn, turned = call_attention(
        functools.partial(forward_kernel, n_head),
        (jax.ShapeDtypeStruct(queries.shape[1:], jnp.bfloat16),) * 2,
        (count, id_column, id_row, queries[0], all_keys, all_vals),
        (seg_len, n_keys),
        2 * pair_flops,
    )

    peer, (attn,) = gate(peer, attn)
    peer_other = [turn(x, "head", 1, "peer_s") for x in peer]
    first_core = me_head == 0
    parts = []
    for s in range(1, n_dp):
        mine, other = peer[s - 1], peer_other[s - 1]
        rows = jnp.concatenate([jnp.where(first_core, mine, other), jnp.where(first_core, other, mine)], 0)
        parts.append(jnp.dot(rows, out_weight, preferred_element_type=jnp.float32).astype(jnp.bfloat16))
    back = [turn(part, "dp", -s, "back") for s, part in zip(range(1, n_dp), parts)]
    own_rows = lax.dynamic_slice(grad_out[0], (0, me_dp * part_rows), (seg_len, part_rows))
    (own_rows,), back = gate([own_rows], *back)
    d_mine = jnp.dot(own_rows, out_weight, preferred_element_type=jnp.float32)
    d_part = jnp.stack(back)

    def backward(d_part):
        return call_attention(
            backward_kernel,
            (
                jax.ShapeDtypeStruct(queries.shape[1:], jnp.bfloat16),
                jax.ShapeDtypeStruct((n_keys, 2 * kv_width), jnp.float32),
            ),
            (count, id_column, id_row, queries[0], all_keys, all_vals, attn, d_mine, d_part, token),
            (seg_len, n_keys),
            5 * pair_flops,
        )


    def send_home(grad_kv):
        sent = []
        for s in range(1, n_ctx):
            begin = seg_len + (s - 1) * SUMMARY_TOKENS
            part = grad_kv[begin : begin + SUMMARY_TOKENS].astype(jnp.bfloat16)
            with jax.named_scope("grads"):
                sent.append(lax.ppermute(part, "ctx", line_pairs(n_ctx, -s)))
        return sent

    def add_home(grad_kv, sent):
        home = sum([x.astype(jnp.float32) for x in sent], grad_kv[cut:seg_len])
        return jnp.concatenate([grad_kv[:cut], home], 0).astype(jnp.bfloat16)

    if wide:
        grad_q, grad_kv = backward(d_part)
        out_kv = add_home(grad_kv, send_home(grad_kv))
        block = d_model // (n_ctx * n_dp)
        columns = (
            grad_out[0].reshape(seg_len, n_dp, n_ctx, block).transpose(0, 2, 1, 3).reshape(seg_len, d_model)
        )
        shard = lax.psum_scatter(
            jnp.einsum("sd,se->de", columns, attn, preferred_element_type=jnp.float32),
            ("ctx", "dp"),
            scatter_dimension=0,
            tiled=True,
        ).astype(jnp.bfloat16)
        weight_grad = lax.all_gather(shard, "ctx", axis=0, tiled=True)
    else:
        steps = range(1, n_dp)
        at_end = (place == 0) | (place == n_ctx - 1)

        def swap(x, name):
            return turn(x, "head", 1, name)

        own_1 = pairs(own, "own")
        own_ma = middle(own_late, "own_a")
        attn_1 = pairs(turned, "attn")
        attn_x0 = [turn(turned, "dp", s, "attn_x0") for s in steps]
        token = mark(token, own_1, own_ma)
        (own_1, own_ma), (token,) = gate([own_1, own_ma], token)
        own_mb = middle(own_1, "own_b")
        own_ea = ends(own_ma, "own_a")
        token = mark(token, own_mb, own_ea)
        (own_mb, attn_0, *peer), (token,) = gate([own_mb, turned, *peer], token)
        own_end = ends(own_mb, "own_b")
        peer_1 = [pairs(x, "peer") for x in peer]
        attn_mid_a = middle(attn_0, "attn_a")
        (attn_1,), (token,) = gate([attn_1], token)
        attn_mid_b = middle(attn_1, "attn_b")
        attn_end_a = ends(attn_mid_a, "attn_a")
        attn_x1 = [turn(attn_1, "dp", s, "attn_x1") for s in steps]
        peer_pair = [jnp.stack([a, b]) for a, b in zip(peer, peer_1)]
        peer_pair, (attn_mid_b, own_end, *rest) = gate(peer_pair, attn_mid_b, own_end, *parts, *attn_x0)
        attn_x0 = rest[n_dp - 1 :]
        attn_end_b = ends(attn_mid_b, "attn_b")
        peer_mid = [middle(x, "peer") for x in peer_pair]
        attn_a = jnp.where(at_end, attn_end_a, attn_mid_a)
        attn_b = jnp.where(at_end, attn_end_b, attn_mid_b)
        attn_xa = [turn(attn_a, "dp", s, "attn_xa") for s in steps]
        attn_xb = [turn(attn_b, "dp", s, "attn_xb") for s in steps]
        peer_1s = [swap(x, "peer_1s") for x in peer_1]
        grad_q, grad_kv = backward(d_part)
        (own_1, own_end), (grad_kv,) = gate([own_1, own_end], grad_kv)
        own_all = jnp.stack([own_1, jnp.where(at_end, own_ea, own_ma), jnp.where(at_end, own_end, own_mb)])
        own_all_s = swap(own_all, "own_s")
        peer_send, (grad_kv, attn_1, *rest) = gate(peer_mid, grad_kv, attn_1, *peer_1s, *attn_x1)
        peer_1s, attn_x1 = rest[: n_dp - 1], rest[n_dp - 1 :]
        peer_end = [ends(x, "peer") for x in peer_send]
        peer_mid_s = [swap(x, "peer_mid_s") for x in peer_send]
        attn_all = jnp.stack([attn_1, attn_a, attn_b])
        share = own_all.shape[0] * half
        rows = jnp.concatenate([own_rows, own_all.reshape(share, -1), own_all_s.reshape(share, -1)], 0)
        cols = [attn, attn_all[:, :half].reshape(share, -1), attn_all[:, half:].reshape(share, -1)]
        total = outer(rows, jnp.concatenate(cols, 0))
        for s in steps:
            rows = [peer[s - 1], peer_other[s - 1], peer_1[s - 1], peer_1s[s - 1]]
            total += outer(jnp.concatenate(rows, 0), jnp.concatenate([attn_x0[s - 1], attn_x1[s - 1]], 0))
        sent = send_home(grad_kv)
        peer_end, (total, *rest) = gate(peer_end, total, *attn_xa, *attn_xb)
        attn_xa, attn_xb = rest[: n_dp - 1], rest[n_dp - 1 :]
        for part, mid, end in ((0, peer_mid, peer_end), (1, peer_mid_s, [swap(x, "peer_end_s") for x in peer_end])):
            for s in steps:
                rows = lax.optimization_barrier(jnp.where(at_end, end[s - 1], mid[s - 1]))
                cols = [x[s - 1][part * half : (part + 1) * half] for x in (attn_xa, attn_xb)]
                total += outer(rows.reshape(2 * half, -1), jnp.concatenate(cols, 0))
        weight_grad = total.astype(jnp.bfloat16)
        sent, (weight_grad,) = gate(sent, weight_grad)
        out_kv = add_home(grad_kv, sent)
    out_k, out_v = out_kv[:, :kv_width], out_kv[:, kv_width:]
    return (grad_q[None], out_k[None], out_v[None], weight_grad)


def solution(mesh):
    placed = (
        P(("groups", "dp"), "ctx", "head"),
        P(("groups", "dp"), "ctx", "head"),
        P(("groups", "dp"), "ctx", "head"),
        P(("groups", "dp"), "ctx"),
        P(("groups", "dp"), "ctx"),
        P("dp", "head"),
        P(("groups", "dp"), "ctx", None),
    )
    return jax.shard_map(
        shards,
        mesh=mesh,
        in_specs=placed,
        out_specs=(
            P(("groups", "dp"), "ctx", "head"),
            P(("groups", "dp"), "ctx", "head"),
            P(("groups", "dp"), "ctx", "head"),
            P(("groups", "dp"), "head"),
        ),
        check_vma=False,
    )
```
